32 devices in a mesh: gx: 4 (over z), gy: 8 (over y, x, core).
Axes of the slice: x: 2, y: 2, z: 4, core: 2. Of those that a mesh axis runs over, the one named last changes fastest.
Arguments:
- face_pieces: bfloat16 [4, 8, 4, 384, 512], P('gx', 'gy'), may hold values from -6 to 6
- edge_pieces: bfloat16 [4, 8, 4, 128, 512], P('gx', 'gy'), may hold values from -6 to 6
- face_counts: int32 [4, 8, 4], P('gx', 'gy'), may hold values from 0 to 6, as said below
- edge_counts: int32 [4, 8, 4], P('gx', 'gy'), may hold values from 0 to 2, as said below
- schur_inv: bfloat16 [4, 8, 2048, 2048], P('gx', 'gy'), may hold values from -0.125 to 0.125
- coarse_basis: bfloat16 [4, 8, 2048, 128], P('gx', 'gy'), may hold values from -0.125 to 0.125
- coarse_mat: float32 [4, 8, 128, 128], P('gx', 'gy'), as said below
- lift_one: float32 [4, 8, 128, 128], P('gx', 'gy'), as said below
- lift_two: float32 [4, 8, 128, 128], P('gx', 'gy'), as said below
Outputs:
- preconditioned_faces: bfloat16 [4, 8, 4, 384, 512], P('gx', 'gy')
- preconditioned_edges: bfloat16 [4, 8, 4, 128, 512], P('gx', 'gy')
The draws below stay inside these ranges and needn't reach their ends.
Inputs may be any that keep to these rules, and one draw needn't show every extreme that they name: face_counts[i, j, k] is the number of live 64-row blocks in face slot k; it is equal at both owners of the face, 0 exactly where an owner lies outside the grid, and 6 is reached in every draw. edge_counts[i, j, k] is the number of live 64-row blocks in edge slot k; it is equal at all four owners of the edge, 0 exactly where some owner lies outside the grid, and 2 is reached in every draw. `coarse_mat`: every block is symmetric positive definite. `lift_one`: every block is nonsingular. `lift_two`: every block is nonsingular, and the blocks of subdomains (i, 2m) and (i, 2m + 1) are equal.
All inputs are finite; a program needn't handle non-finite values.
Results may differ from the reference program's by a relative error of at most 0.0062.
Values may be sent and summed in bfloat16 or wider, within the bound.
A program may use at most 128 MiB of HBM per device.

```python
import math
import jax
import jax.numpy as jnp
from jax import lax

ROWS = 64
MAXB = 6
EMAXB = 2
NVEC = 512
NC = 128
FR = 384
ER = 128
NI = 2048
SGX = 4
SGY = 8


def draw_face_counts(key, part):
    row_key, column_key = jax.random.split(jax.random.fold_in(key, 11))
    faces_rows = jax.random.randint(row_key, (SGX - 1, SGY), 1, MAXB + 1)
    faces_rows = faces_rows.at[0, 0].set(MAXB)
    faces_cols = jax.random.randint(column_key, (SGX, SGY - 1), 1, MAXB + 1)
    padded_rows = jnp.pad(faces_rows, ((1, 1), (0, 0)))
    padded_cols = jnp.pad(faces_cols, ((0, 0), (1, 1)))
    stacked = jnp.stack([padded_rows[:-1], padded_cols[:, :-1], padded_cols[:, 1:], padded_rows[1:]], axis=-1)
    return stacked.astype(jnp.int32)


def draw_edge_counts(key, part):
    edge_key = jax.random.fold_in(key, 13)
    edge_points = jax.random.randint(edge_key, (SGX - 1, SGY - 1), 1, EMAXB + 1)
    edge_points = edge_points.at[0, 0].set(EMAXB)
    padded_edges = jnp.pad(edge_points, ((1, 1), (1, 1)))
    stacked = jnp.stack([padded_edges[:-1, :-1], padded_edges[:-1, 1:], padded_edges[1:, :-1], padded_edges[1:, 1:]], axis=-1)
    return stacked.astype(jnp.int32)


def draw_coarse_mat(key, part):
    diag_key, spread_key = jax.random.split(jax.random.fold_in(key, 23))
    diagonal = jax.random.uniform(diag_key, (SGX, SGY, NC), jnp.float32, 1.0, 3.0)
    off_diag = jnp.clip(0.5 * jax.random.normal(spread_key, (SGX, SGY, NC, NC), jnp.float32), -1.0, 1.0)
    identity = jnp.eye(NC, dtype=jnp.float32)
    off_diag = (off_diag + jnp.swapaxes(off_diag, -1, -2)) * (0.5 / NC) * (1.0 - identity)
    return (off_diag + diagonal[..., None] * identity) / SGY


def lift_draw(key, salt, columns):
    diag_key, spread_key = jax.random.split(jax.random.fold_in(key, salt))
    diagonal = jax.random.uniform(diag_key, (SGX, columns, NC), jnp.float32, 0.8, 1.25)
    off_diag = jax.random.normal(spread_key, (SGX, columns, NC, NC), jnp.float32) * (0.25 / math.sqrt(NC))
    return off_diag + diagonal[..., None] * jnp.eye(NC, dtype=jnp.float32)


def draw_lift_one(key, part):
    return lift_draw(key, 31, SGY)


def draw_lift_two(key, part):
    node_blocks = lift_draw(key, 47, SGY // 2)
    return jnp.repeat(node_blocks, 2, axis=1)


def levels(key, extent, shards, low, high):
    level = 1.0
    for position, parts in shards:
        draws = jax.random.uniform(jax.random.fold_in(jax.random.fold_in(key, 6), position), (parts,), jnp.float32, low / len(shards), high / len(shards))
        level = level * jnp.repeat(jnp.exp(draws), extent[position] // parts).reshape((-1,) + (1,) * (len(extent) - 1 - position))
    return level


def centred(rng, shape, deviation, most, cuts=(), held_as=jnp.bfloat16):
    level = levels(rng, shape, cuts, -0.22, 0.18) if cuts else 1.0
    result = jax.random.normal(rng, shape, jnp.float32) * deviation * level
    return jnp.minimum(jnp.maximum(result, -most), most).astype(held_as)


def setup_inputs(seed: int = 0) -> dict:
    key_of = jax.random.split(jax.random.key(seed), 10)
    return {
        "face_pieces": centred(key_of[0], (SGX, SGY, 4, FR, NVEC), 1.0, 6.0, ((0, 4), (1, 8))),
        "edge_pieces": centred(key_of[1], (SGX, SGY, 4, ER, NVEC), 1.0, 6.0, ((0, 4), (1, 8))),
        "face_counts": draw_face_counts(jax.random.fold_in(key_of[9], 71), 0),
        "edge_counts": draw_edge_counts(jax.random.fold_in(key_of[9], 71), 0),
        "schur_inv": centred(key_of[4], (SGX, SGY, NI, NI), NI ** -0.5, 0.125, ((0, 4), (1, 8))),
        "coarse_basis": centred(key_of[5], (SGX, SGY, NI, NC), NI ** -0.5, 0.125, ((0, 4), (1, 8))),
        "coarse_mat": draw_coarse_mat(jax.random.fold_in(key_of[9], 71), 0),
        "lift_one": draw_lift_one(jax.random.fold_in(key_of[9], 71), 0),
        "lift_two": draw_lift_two(jax.random.fold_in(key_of[9], 71), 0),
    }


def widen(values):
    return values.astype(jnp.float32)

def owner_sums(faces, edges):
    face_pad = jnp.pad(faces, ((1, 1), (1, 1), (0, 0), (0, 0), (0, 0)))
    edge_pad = jnp.pad(edges, ((1, 1), (1, 1), (0, 0), (0, 0), (0, 0)))
    face_rows = []
    edge_rows = []
    for row_index in range(SGX):
        upper = face_pad[row_index]
        middle = face_pad[row_index + 1]
        lower = face_pad[row_index + 2]
        face_terms = jnp.stack([widen(upper[1:-1, 3]), widen(middle[:-2, 2]), widen(middle[2:, 1]), widen(lower[1:-1, 0])], axis=1)
        face_rows.append(widen(faces[row_index]) + face_terms)
        eu = edge_pad[row_index]
        em = edge_pad[row_index + 1]
        ed = edge_pad[row_index + 2]
        north_west = widen(em[:-2, 1]) + widen(eu[1:-1, 2]) + widen(eu[:-2, 3])
        north_east = widen(em[2:, 0]) + widen(eu[1:-1, 3]) + widen(eu[2:, 2])
        south_west = widen(em[:-2, 3]) + widen(ed[1:-1, 0]) + widen(ed[:-2, 1])
        south_east = widen(em[2:, 2]) + widen(ed[1:-1, 1]) + widen(ed[2:, 0])
        edge_rows.append(widen(edges[row_index]) + jnp.stack([north_west, north_east, south_west, south_east], axis=1))
    return (jnp.stack(face_rows), jnp.stack(edge_rows))

def reference(face_pieces, edge_pieces, face_counts, edge_counts, schur_inv, coarse_basis, coarse_mat, lift_one, lift_two):
    highest = lax.Precision.HIGHEST
    contract_first = (((0,), (0,)), ((), ()))
    face_len = face_pieces.shape[3]
    edge_len = edge_pieces.shape[3]
    face_live = (jnp.arange(face_len, dtype=jnp.int32)[None, None, None, :, None] < (face_counts * ROWS)[..., None, None]).astype(jnp.float32)
    edge_live = (jnp.arange(edge_len, dtype=jnp.int32)[None, None, None, :, None] < (edge_counts * ROWS)[..., None, None]).astype(jnp.float32)
    face_sum, edge_sum = owner_sums(face_pieces, edge_pieces)
    face_res = (face_sum * face_live * 0.5).astype(jnp.bfloat16)
    edge_res = (edge_sum * edge_live * 0.25).astype(jnp.bfloat16)
    flat_rhs = jnp.concatenate([face_res.reshape(SGX, SGY, 4 * face_len, NVEC), edge_res.reshape(SGX, SGY, 4 * edge_len, NVEC)], axis=2)

    def child_terms(node_basis, rhs_block, child_matrix, first_lift):
        coarse_rhs = lax.dot_general(node_basis.astype(jnp.float32), rhs_block.astype(jnp.float32), contract_first, precision=highest)
        moved = jnp.dot(child_matrix, first_lift, precision=highest)
        child_term = lax.dot_general(first_lift, moved, contract_first, precision=highest)
        child_rhs = lax.dot_general(first_lift, coarse_rhs, contract_first, precision=highest)
        return jnp.concatenate([child_term, child_rhs], axis=1)
    terms = jax.vmap(jax.vmap(child_terms))(coarse_basis, flat_rhs, coarse_mat, lift_one)
    pair_view = terms.reshape(SGX, SGY // 2, 2, NC, NC + NVEC)
    pair_total = jnp.broadcast_to(jnp.sum(pair_view, axis=2, keepdims=True), pair_view.shape).reshape(terms.shape)

    def lift_pair(pair_data, second_lift):
        moved = jnp.dot(pair_data[:, :NC], second_lift, precision=highest)
        row_term = lax.dot_general(second_lift, moved, contract_first, precision=highest)
        row_rhs = lax.dot_general(second_lift, pair_data[:, NC:], contract_first, precision=highest)
        return jnp.concatenate([row_term, row_rhs], axis=1)
    level_terms = jax.vmap(jax.vmap(lift_pair))(pair_total, lift_two)
    row_totals = jnp.sum(0.5 * level_terms, axis=1)

    def solve_row(row_total):
        factor = jnp.linalg.cholesky(row_total[:, :NC])
        return jax.scipy.linalg.cho_solve((factor, True), row_total[:, NC:])
    coarse_solution = jax.vmap(solve_row)(row_totals)

    def correct(local_inverse, node_basis, rhs_block, first_lift, second_lift, solution):
        middle_values = jnp.dot(second_lift, solution, precision=highest)
        node_values = jnp.dot(first_lift, middle_values, precision=highest).astype(jnp.bfloat16)
        coarse_part = jnp.dot(node_basis.astype(jnp.float32), node_values.astype(jnp.float32), precision=highest)
        local_part = jnp.dot(local_inverse.astype(jnp.float32), rhs_block.astype(jnp.float32), precision=highest)
        return (local_part + coarse_part).astype(jnp.bfloat16)

    def correct_row(row_args):
        local_inverse, node_basis, rhs_block, first_lift, second_lift, solution = row_args
        return jax.vmap(correct, in_axes=(0, 0, 0, 0, 0, None))(local_inverse, node_basis, rhs_block, first_lift, second_lift, solution)
    corrected = lax.map(correct_row, (schur_inv, coarse_basis, flat_rhs, lift_one, lift_two, coarse_solution))
    face_corr = corrected[:, :, :4 * face_len].reshape(SGX, SGY, 4, face_len, NVEC)
    edge_corr = corrected[:, :, 4 * face_len:].reshape(SGX, SGY, 4, edge_len, NVEC)
    face_out, edge_out = owner_sums(face_corr, edge_corr)
    return ((face_out * 0.5 * face_live).astype(jnp.bfloat16), (edge_out * 0.25 * edge_live).astype(jnp.bfloat16))
```

```python
import functools

import jax
import jax.numpy as jnp
from jax import lax
from jax.experimental import pallas as pl
from jax.experimental.pallas import tpu as pltpu
from jax.sharding import PartitionSpec as P

ROWS = 64
F32 = jnp.float32
BF16 = jnp.bfloat16
MESH = pl.DeviceIdType.MESH
HIGHEST = lax.Precision.HIGHEST
FACE_STEP = ((-1, 0), (0, -1), (0, 1), (1, 0))
EDGE_STEP = ((-1, -1), (-1, 1), (1, -1), (1, 1))
COLS0 = (((0,), (0,)), ((), ()))


def exact_dot(a, b):
    return jnp.dot(a, b, precision=HIGHEST, preferred_element_type=F32)


def exact_dot_t(a, b):
    return lax.dot_general(a, b, COLS0, precision=HIGHEST, preferred_element_type=F32)


def invert(matrix):
    size = matrix.shape[0]
    block = 8
    lane = lax.broadcasted_iota(jnp.int32, (1, size), 1)
    row = lax.broadcasted_iota(jnp.int32, (size, 1), 0)

    def step(_, a):
        for p in range(0, block, 2):
            q = p + 1
            r0, r1 = a[p : p + 1, :], a[q : q + 1, :]
            c0, c1 = a[:, p : p + 1], a[:, q : q + 1]
            d00, d01 = a[p : p + 1, p : p + 1], a[p : p + 1, q : q + 1]
            d10, d11 = a[q : q + 1, p : p + 1], a[q : q + 1, q : q + 1]
            inv = 1.0 / (d00 * d11 - d01 * d10)
            e0 = jnp.where(lane == p, 1.0, 0.0)
            e1 = jnp.where(lane == q, 1.0, 0.0)
            pivot_lane = (lane == p) | (lane == q)
            pivot_row = (row == p) | (row == q)
            r0 = jnp.where(pivot_lane, e0, r0)
            r1 = jnp.where(pivot_lane, e1, r1)
            w0 = (d11 * inv) * r0 - (d01 * inv) * r1
            w1 = (d00 * inv) * r1 - (d10 * inv) * r0
            c0 = jnp.where(pivot_row, jnp.where(row == p, -1.0, 0.0), c0)
            c1 = jnp.where(pivot_row, jnp.where(row == q, -1.0, 0.0), c1)
            a = jnp.where(pivot_row | pivot_lane, 0.0, a) - c0 * w0 - c1 * w1
        a = jnp.concatenate([a[block:], a[:block]], axis=0)
        return pltpu.roll(a, size - block, 1)

    return lax.fori_loop(0, size // block, step, matrix)


def kernel(
    gx,
    gy,
    rows,
    faces_hbm,
    edges_hbm,
    fcnt,
    ecnt,
    schur_hbm,
    basis_hbm,
    cmat_hbm,
    l1_hbm,
    l2_hbm,
    outf_hbm,
    oute_hbm,
    faces,
    edges,
    schur,
    basis,
    cmat,
    l1,
    l2,
    rf,
    e1,
    e2,
    e3,
    cs,
    res,
    acc,
    corr,
    out,
    mpart,
    mslots,
    mfull,
    bpart,
    bslots,
    bfull,
    local_sem,
    fsend,
    frecv,
    esend,
    erecv,
    csend,
    crecv,
    osem,
):
    i = lax.axis_index("gx")
    j = lax.axis_index("gy")
    fr = faces.shape[1]
    er = edges.shape[1]
    half = er // 2
    nc = mpart.shape[0]
    owners = nc // rows

    locals_ = [
        pltpu.make_async_copy(src, dst, local_sem.at[n])
        for n, (src, dst) in enumerate(
            (
                (l1_hbm, l1),
                (l2_hbm, l2),
                (cmat_hbm, cmat),
                (edges_hbm, edges),
                (faces_hbm, faces),
                (basis_hbm, basis),
                (schur_hbm, schur),
            )
        )
    ]
    for copy in locals_:
        copy.start()

    has = {-1: i > 0, 1: i < gx - 1}
    hasy = {-1: j > 0, 1: j < gy - 1}

    def peer(d):
        return lax.rem(j + d, gy)

    barrier = pltpu.get_barrier_semaphore()
    for d in range(1, gy):
        pl.semaphore_signal(barrier, inc=1, device_id=(i, peer(d)), device_id_type=MESH)
    for a in (-1, 1):

        @pl.when(has[a])
        def _():
            pl.semaphore_signal(barrier, inc=1, device_id=(i + a, j), device_id_type=MESH)

    pl.semaphore_wait(barrier, gy - 1 + has[-1].astype(jnp.int32) + has[1].astype(jnp.int32))

    def remote(src, dst, ssem, rsem, target):
        return pltpu.make_async_remote_copy(
            src_ref=src,
            dst_ref=dst,
            send_sem=ssem,
            recv_sem=rsem,
            device_id=target,
            device_id_type=MESH,
        )

    def face_has(k):
        a, b = FACE_STEP[k]
        return has[a] if a else hasy[b]

    def face_copy(ph, k, src):
        a, b = FACE_STEP[k]
        return remote(src, rf.at[ph, 3 - k], fsend.at[ph, k], frecv.at[ph, 3 - k], (i + a, j + b))

    def face_arrival(ph, k):
        a, b = FACE_STEP[k]
        return remote(rf.at[ph, k], rf.at[ph, k], fsend.at[ph, k], frecv.at[ph, k], (i + a, j + b))

    def edge_has(s):
        a, b = EDGE_STEP[s]
        return has[a] & hasy[b]

    def mine(s):
        return 0 if s % 2 else half

    def edge_copy(ph, stage, s, src):
        a, b = EDGE_STEP[s]
        land, flip, target = (
            (e1, s ^ 1, (i, j + b)),
            (e2, s ^ 2, (i + a, j)),
            (e3, s ^ 1, (i, j + b)),
        )[stage]
        return remote(
            src, land.at[ph, flip], esend.at[ph, stage, s], erecv.at[ph, stage, flip], target
        )

    def edge_arrival(ph, stage, s):
        a, b = EDGE_STEP[s]
        land = (e1, e2, e3)[stage]
        target = (i + a, j) if stage == 1 else (i, j + b)
        ref = land.at[ph, s]
        return remote(ref, ref, esend.at[ph, stage, s], erecv.at[ph, stage, s], target)

    def owned_by(index):
        return True if owners >= gy else index < owners

    def guarded(cond, fn):
        if cond is True:
            fn()
        else:
            pl.when(cond)(fn)

    def part_rows(ref, index):
        return ref.at[pl.ds(pl.multiple_of(index * rows, rows), rows)]

    def scatter_copy(which, src, slots, d):
        p = peer(d)
        return remote(
            part_rows(src, jnp.minimum(p, owners - 1)), slots.at[d], csend.at[which, d], crecv.at[which, d], (i, p)
        )

    def scatter_start(which, src, slots):
        for d in range(1, gy):
            guarded(owned_by(peer(d)), lambda: scatter_copy(which, src, slots, d).start())

    def gather_copy(which, full, d):
        ref = part_rows(full, jnp.minimum(j, owners - 1))
        return remote(ref, ref, csend.at[which, d], crecv.at[which, d], (i, peer(d)))

    def sum_and_gather(which, src, slots, full):
        def go():
            total = part_rows(src, jnp.minimum(j, owners - 1))[...]
            for d in range(1, gy):
                scatter_copy(which, src, slots, d).wait_recv()
                total = total + slots[d]
            part_rows(full, jnp.minimum(j, owners - 1))[...] = total
            for d in range(1, gy):
                gather_copy(which + 1, full, d).start()

        guarded(owned_by(j), go)

    def gather_wait(which, full):
        for d in range(1, gy):
            q = lax.rem(j - d + gy, gy)

            def wait():
                ref = part_rows(full, jnp.minimum(q, owners - 1))
                remote(ref, ref, csend.at[which, d], crecv.at[which, d], (i, q)).wait_recv()

            guarded(owned_by(q), wait)

    def collective_drain(which, src, slots, full):
        for d in range(1, gy):
            guarded(owned_by(peer(d)), lambda: scatter_copy(which, src, slots, d).wait_send())
            guarded(owned_by(j), lambda: gather_copy(which + 1, full, d).wait_send())

    def edge_halves_start(ph, src):
        for s in range(4):

            @pl.when(edge_has(s))
            def _():
                edge_copy(ph, 0, s, src.at[s, pl.ds(half - mine(s), half)]).start()

    def edge_columns(ph, own):
        for s in range(4):

            @pl.when(edge_has(s))
            def _():
                edge_arrival(ph, 0, s).wait_recv()
                total = own[s, pl.ds(mine(s), half)].astype(F32) + e1[ph, s].astype(F32)
                cs[ph, s] = total.astype(BF16)
                edge_copy(ph, 1, s, cs.at[ph, s]).start()

    def edge_totals(ph, own, dst):
        for s in range(4):
            rows_ref = dst.at[pl.ds(4 * fr + s * er + mine(s), half)]

            @pl.when(edge_has(s))
            def _():
                edge_arrival(ph, 1, s).wait_recv()
                total = own[s, pl.ds(mine(s), half)].astype(F32) + e1[ph, s].astype(F32)
                total = total + e2[ph, s].astype(F32)
                for b in range(half // ROWS):
                    block = mine(s) // ROWS + b
                    scale = jnp.where(ecnt[0, 0, s] > block, 0.25, 0.0)
                    part = total[b * ROWS : (b + 1) * ROWS] * scale
                    rows_ref[pl.ds(b * ROWS, ROWS)] = part.astype(BF16)
                edge_copy(ph, 2, s, rows_ref).start()

    def edge_finish(ph, dst):
        for s in range(4):
            base = 4 * fr + s * er

            @pl.when(edge_has(s))
            def _():
                edge_arrival(ph, 2, s).wait_recv()
                dst[pl.ds(base + half - mine(s), half)] = e3[ph, s]

            @pl.when(jnp.logical_not(edge_has(s)))
            def _():
                dst[pl.ds(base, er)] = jnp.zeros((er, dst.shape[1]), BF16)

    def face_finish(ph, k, own, dst):
        @pl.when(face_has(k))
        def _():
            face_arrival(ph, k).wait_recv()
            for b in range(fr // ROWS):
                scale = jnp.where(fcnt[0, 0, k] > b, 0.5, 0.0)
                at = pl.ds(b * ROWS, ROWS)
                total = own[k, at].astype(F32) + rf[ph, k, at].astype(F32)
                dst[pl.ds(k * fr + b * ROWS, ROWS)] = (total * scale).astype(BF16)

        @pl.when(jnp.logical_not(face_has(k)))
        def _():
            dst[pl.ds(k * fr, fr)] = jnp.zeros((fr, dst.shape[1]), BF16)

    edge_halves_start(0, edges_hbm)
    for k in (0, 3, 1, 2):

        @pl.when(face_has(k))
        def _():
            face_copy(0, k, faces_hbm.at[k]).start()

    for n in range(3):
        locals_[n].wait()
    lift = exact_dot(l1[...], l2[...])
    l1[...] = lift
    mpart[...] = exact_dot_t(lift, exact_dot(cmat[...], lift))
    scatter_start(0, mpart, mslots)
    locals_[3].wait()
    edge_columns(0, edges)
    sum_and_gather(0, mpart, mslots, mfull)
    gather_wait(1, mfull)
    mfull_inv = invert(mfull[...])
    collective_drain(0, mpart, mslots, mfull)
    l2[...] = mfull_inv

    locals_[4].wait()
    for k in (1, 2):
        face_finish(0, k, faces, res)
    edge_totals(0, edges, res)
    for k in (0, 3):
        face_finish(0, k, faces, res)
    edge_finish(0, res)

    locals_[5].wait()
    coarse = lax.dot_general(basis[...], res[...], COLS0, preferred_element_type=F32)
    bpart[...] = exact_dot_t(l1[...], coarse)
    scatter_start(2, bpart, bslots)
    locals_[6].wait()

    def local_solve(base, count):
        at = pl.ds(pl.multiple_of(base, 128), count)
        acc[at] = jnp.dot(schur[at], res[...], preferred_element_type=F32)

    @pl.loop(0, 2)
    def _(t):
        local_solve(t * (3 * fr), fr)

    sum_and_gather(2, bpart, bslots, bfull)

    @pl.loop(0, 3)
    def _(t):
        local_solve(jnp.where(t == 0, 4 * fr, t * fr), fr)

    local_solve(5 * fr, 4 * er - fr)

    gather_wait(3, bfull)
    middle = exact_dot(l2[...], bfull[...])
    node = exact_dot(l1[...], middle).astype(BF16)

    def add_coarse(base, count):
        at = pl.ds(base, count)
        return (acc[at] + jnp.dot(basis[at], node, preferred_element_type=F32)).astype(BF16)

    for s in range(4):
        edges[s] = add_coarse(4 * fr + s * er, er)
    for k in (0, 3, 1, 2):
        corr[k] = add_coarse(k * fr, fr)
        if k == 0:
            for s in range(4):

                @pl.when(edge_has(s))
                def _():
                    edge_copy(0, 0, s, edges_hbm.at[s, pl.ds(half - mine(s), half)]).wait_send()

            edge_halves_start(1, edges)

        @pl.when(face_has(k))
        def _():
            face_copy(1, k, corr.at[k]).start()

    edge_columns(1, edges)

    def put_face(k):
        return pltpu.make_async_copy(out.at[pl.ds(k * fr, fr)], outf_hbm.at[k], osem.at[k])

    def put_edge(s):
        return pltpu.make_async_copy(
            out.at[pl.ds(4 * fr + s * er, er)], oute_hbm.at[s], osem.at[4 + s]
        )

    for k in (1, 2):
        face_finish(1, k, corr, out)
        put_face(k).start()
    edge_totals(1, edges, out)
    for k in (0, 3):
        face_finish(1, k, corr, out)
        put_face(k).start()
    edge_finish(1, out)
    for s in range(4):
        put_edge(s).start()

    collective_drain(2, bpart, bslots, bfull)
    for ph in range(2):
        for k in range(4):

            @pl.when(face_has(k))
            def _():
                face_copy(ph, k, faces_hbm.at[k] if ph == 0 else corr.at[k]).wait_send()

        for s in range(4):

            @pl.when(edge_has(s))
            def _():
                if ph:
                    edge_copy(1, 0, s, edges.at[s, pl.ds(half - mine(s), half)]).wait_send()
                edge_copy(ph, 1, s, cs.at[ph, s]).wait_send()
                edge_copy(
                    ph, 2, s, (out if ph else res).at[pl.ds(4 * fr + s * er + mine(s), half)]
                ).wait_send()

    for k in range(4):
        put_face(k).wait()
        put_edge(k).wait()


def body(
    face_pieces,
    edge_pieces,
    face_counts,
    edge_counts,
    schur_inv,
    coarse_basis,
    coarse_mat,
    lift_one,
    lift_two,
):
    gx, gy = lax.axis_size("gx"), lax.axis_size("gy")
    faces, edges = face_pieces[0, 0], edge_pieces[0, 0]
    fr, vec = faces.shape[1:]
    er = edges.shape[1]
    ni, nc = coarse_basis.shape[2:]
    rows = max(16, nc // gy)
    half = er // 2
    anywhere = pl.BlockSpec(memory_space=pl.ANY)
    smem = pl.BlockSpec(memory_space=pltpu.SMEM)
    dma = pltpu.SemaphoreType.DMA
    out_faces, out_edges = pl.pallas_call(
        functools.partial(kernel, gx, gy, rows),
        out_shape=(
            jax.ShapeDtypeStruct(faces.shape, BF16),
            jax.ShapeDtypeStruct(edges.shape, BF16),
        ),
        in_specs=[anywhere, anywhere, smem, smem] + [anywhere] * 5,
        out_specs=(anywhere, anywhere),
        scratch_shapes=[
            pltpu.VMEM(faces.shape, BF16),
            pltpu.VMEM(edges.shape, BF16),
            pltpu.VMEM((ni, ni), BF16),
            pltpu.VMEM((ni, nc), BF16),
            pltpu.VMEM((nc, nc), F32),
            pltpu.VMEM((nc, nc), F32),
            pltpu.VMEM((nc, nc), F32),
            pltpu.VMEM((2, 4, fr, vec), BF16),
            pltpu.VMEM((2, 4, half, vec), BF16),
            pltpu.VMEM((2, 4, half, vec), BF16),
            pltpu.VMEM((2, 4, half, vec), BF16),
            pltpu.VMEM((2, 4, half, vec), BF16),
            pltpu.VMEM((ni, vec), BF16),
            pltpu.VMEM((ni, vec), F32),
            pltpu.VMEM(faces.shape, BF16),
            pltpu.VMEM((ni, vec), BF16),
            pltpu.VMEM((nc, nc), F32),
            pltpu.VMEM((gy, rows, nc), F32),
            pltpu.VMEM((nc, nc), F32),
            pltpu.VMEM((nc, vec), F32),
            pltpu.VMEM((gy, rows, vec), F32),
            pltpu.VMEM((nc, vec), F32),
            dma((7,)),
            dma((2, 4)),
            dma((2, 4)),
            dma((2, 3, 4)),
            dma((2, 3, 4)),
            dma((4, gy)),
            dma((4, gy)),
            dma((8,)),
        ],
        compiler_params=pltpu.CompilerParams(
            collective_id=0, has_side_effects=True, vmem_limit_bytes=52 * 2**20
        ),
        cost_estimate=pl.CostEstimate(
            flops=2 * ni * vec * (ni + 2 * nc), bytes_accessed=2 * ni * (ni + 3 * vec), transcendentals=0
        ),
    )(
        faces,
        edges,
        face_counts,
        edge_counts,
        schur_inv[0, 0],
        coarse_basis[0, 0],
        coarse_mat[0, 0],
        lift_one[0, 0],
        lift_two[0, 0],
    )
    return out_faces[None, None], out_edges[None, None]


def solution(mesh):
    return jax.shard_map(
        body,
        mesh=mesh,
        in_specs=(
            P("gx", "gy", None, None, None),
            P("gx", "gy", None, None, None),
            P("gx", "gy", None),
            P("gx", "gy", None),
            P("gx", "gy", None, None),
            P("gx", "gy", None, None),
            P("gx", "gy", None, None),
            P("gx", "gy", None, None),
            P("gx", "gy", None, None),
        ),
        out_specs=(P("gx", "gy", None, None, None), P("gx", "gy", None, None, None)),
        check_vma=False,
    )
```

```python
import functools

import jax
import jax.numpy as jnp
from jax import lax
from jax.experimental import pallas as pl
from jax.experimental.pallas import tpu as pltpu
from jax.sharding import PartitionSpec as P

ROWS = 64
F32 = jnp.float32
BF16 = jnp.bfloat16
MESH = pl.DeviceIdType.MESH
HIGHEST = lax.Precision.HIGHEST
FACE_STEP = ((-1, 0), (0, -1), (0, 1), (1, 0))
EDGE_STEP = ((-1, -1), (-1, 1), (1, -1), (1, 1))
COLS0 = (((0,), (0,)), ((), ()))


def exact_dot(a, b):
    return jnp.dot(a, b, precision=HIGHEST, preferred_element_type=F32)


def exact_dot_t(a, b):
    return lax.dot_general(a, b, COLS0, precision=HIGHEST, preferred_element_type=F32)


def invert(matrix):
    size = matrix.shape[0]
    block = 8
    lane = lax.broadcasted_iota(jnp.int32, (1, size), 1)

    def step(_, a):
        cols = [jnp.broadcast_to(a[:, t : t + 1], (size, size)) for t in range(block)]
        d = [[cols[t][s : s + 1] for t in range(block)] for s in range(block)]
        w = [
            jnp.where(lane < block, jnp.where(lane == s, 1.0, 0.0), a[s : s + 1])
            for s in range(block)
        ]
        for p in range(0, block, 2):
            q = p + 1
            inv = 1.0 / (d[p][p] * d[q][q] - d[p][q] * d[q][p])
            i00, i01 = d[q][q] * inv, d[p][q] * inv
            i10, i11 = d[q][p] * inv, d[p][p] * inv
            w[p], w[q] = i00 * w[p] - i01 * w[q], i11 * w[q] - i10 * w[p]
            for t in range(q + 1, block):
                d[p][t], d[q][t] = i00 * d[p][t] - i01 * d[q][t], i11 * d[q][t] - i10 * d[p][t]
            for s in range(block):
                if s not in (p, q):
                    f, g = d[s][p], d[s][q]
                    w[s] = w[s] - f * w[p] - g * w[q]
                    for t in range(q + 1, block):
                        d[s][t] = d[s][t] - f * d[p][t] - g * d[q][t]
        rest = jnp.where(lane < block, 0.0, a[block:])
        for t in range(block):
            rest = rest - cols[t][block:] * w[t]
        return pltpu.roll(jnp.concatenate([rest] + w, axis=0), size - block, 1)

    return lax.fori_loop(0, size // block, step, matrix)


def kernel(
    gx,
    gy,
    rows,
    faces_hbm,
    edges_hbm,
    fcnt,
    ecnt,
    schur_hbm,
    basis_hbm,
    cmat_hbm,
    l1_hbm,
    l2_hbm,
    outf_hbm,
    oute_hbm,
    faces,
    edges,
    schur,
    basis,
    cmat,
    l1,
    l2,
    rf,
    e1,
    e2,
    e3,
    cs,
    res,
    acc,
    corr,
    out,
    mpart,
    mslots,
    mfull,
    bpart,
    bslots,
    bfull,
    local_sem,
    fsend,
    frecv,
    esend,
    erecv,
    csend,
    crecv,
    osem,
):
    i = lax.axis_index("gx")
    j = lax.axis_index("gy")
    fr = faces.shape[1]
    er = edges.shape[1]
    half = er // 2
    nc = mpart.shape[0]
    owners = nc // rows

    locals_ = [
        pltpu.make_async_copy(src, dst, local_sem.at[n])
        for n, (src, dst) in enumerate(
            (
                (l1_hbm, l1),
                (l2_hbm, l2),
                (cmat_hbm, cmat),
                (edges_hbm, edges),
                (faces_hbm, faces),
                (basis_hbm, basis),
                (schur_hbm, schur),
            )
        )
    ]
    for copy in locals_:
        copy.start()

    has = {-1: i > 0, 1: i < gx - 1}
    hasy = {-1: j > 0, 1: j < gy - 1}

    def peer(d):
        return lax.rem(j + d, gy)

    barrier = pltpu.get_barrier_semaphore()
    for d in range(1, gy):
        pl.semaphore_signal(barrier, inc=1, device_id=(i, peer(d)), device_id_type=MESH)
    for a in (-1, 1):

        @pl.when(has[a])
        def _():
            pl.semaphore_signal(barrier, inc=1, device_id=(i + a, j), device_id_type=MESH)

    pl.semaphore_wait(barrier, gy - 1 + has[-1].astype(jnp.int32) + has[1].astype(jnp.int32))

    def remote(src, dst, ssem, rsem, target):
        return pltpu.make_async_remote_copy(
            src_ref=src,
            dst_ref=dst,
            send_sem=ssem,
            recv_sem=rsem,
            device_id=target,
            device_id_type=MESH,
        )

    def face_has(k):
        a, b = FACE_STEP[k]
        return has[a] if a else hasy[b]

    def face_copy(ph, k, src):
        a, b = FACE_STEP[k]
        return remote(src, rf.at[ph, 3 - k], fsend.at[ph, k], frecv.at[ph, 3 - k], (i + a, j + b))

    def face_arrival(ph, k):
        a, b = FACE_STEP[k]
        return remote(rf.at[ph, k], rf.at[ph, k], fsend.at[ph, k], frecv.at[ph, k], (i + a, j + b))

    def edge_has(s):
        a, b = EDGE_STEP[s]
        return has[a] & hasy[b]

    def mine(s):
        return 0 if s % 2 else half

    def edge_copy(ph, stage, s, src):
        a, b = EDGE_STEP[s]
        land, flip, target = (
            (e1, s ^ 1, (i, j + b)),
            (e2, s ^ 2, (i + a, j)),
            (e3, s ^ 1, (i, j + b)),
        )[stage]
        return remote(
            src, land.at[ph, flip], esend.at[ph, stage, s], erecv.at[ph, stage, flip], target
        )

    def edge_arrival(ph, stage, s):
        a, b = EDGE_STEP[s]
        land = (e1, e2, e3)[stage]
        target = (i + a, j) if stage == 1 else (i, j + b)
        ref = land.at[ph, s]
        return remote(ref, ref, esend.at[ph, stage, s], erecv.at[ph, stage, s], target)

    def owned_by(index):
        return True if owners >= gy else index < owners

    def guarded(cond, fn):
        if cond is True:
            fn()
        else:
            pl.when(cond)(fn)

    def part_rows(ref, index):
        return ref.at[pl.ds(pl.multiple_of(index * rows, rows), rows)]

    def scatter_copy(which, src, slots, d):
        p = peer(d)
        return remote(
            part_rows(src, jnp.minimum(p, owners - 1)), slots.at[d], csend.at[which, d], crecv.at[which, d], (i, p)
        )

    def scatter_start(which, src, slots):
        for d in range(1, gy):
            guarded(owned_by(peer(d)), lambda: scatter_copy(which, src, slots, d).start())

    def gather_copy(which, full, d):
        ref = part_rows(full, jnp.minimum(j, owners - 1))
        return remote(ref, ref, csend.at[which, d], crecv.at[which, d], (i, peer(d)))

    def sum_and_gather(which, src, slots, full):
        def go():
            total = part_rows(src, jnp.minimum(j, owners - 1))[...]
            for d in range(1, gy):
                scatter_copy(which, src, slots, d).wait_recv()
                total = total + slots[d]
            part_rows(full, jnp.minimum(j, owners - 1))[...] = total
            for d in range(1, gy):
                gather_copy(which + 1, full, d).start()

        guarded(owned_by(j), go)

    def gather_wait(which, full):
        for d in range(1, gy):
            q = lax.rem(j - d + gy, gy)

            def wait():
                ref = part_rows(full, jnp.minimum(q, owners - 1))
                remote(ref, ref, csend.at[which, d], crecv.at[which, d], (i, q)).wait_recv()

            guarded(owned_by(q), wait)

    def collective_drain(which, src, slots, full):
        for d in range(1, gy):
            guarded(owned_by(peer(d)), lambda: scatter_copy(which, src, slots, d).wait_send())
            guarded(owned_by(j), lambda: gather_copy(which + 1, full, d).wait_send())

    def edge_halves_start(ph, src):
        for s in range(4):

            @pl.when(edge_has(s))
            def _():
                edge_copy(ph, 0, s, src.at[s, pl.ds(half - mine(s), half)]).start()

    def edge_columns(ph, own):
        for s in range(4):

            @pl.when(edge_has(s))
            def _():
                edge_arrival(ph, 0, s).wait_recv()
                total = own[s, pl.ds(mine(s), half)].astype(F32) + e1[ph, s].astype(F32)
                cs[ph, s] = total.astype(BF16)
                edge_copy(ph, 1, s, cs.at[ph, s]).start()

    def edge_totals(ph, own, dst):
        for s in range(4):
            rows_ref = dst.at[pl.ds(4 * fr + s * er + mine(s), half)]

            @pl.when(edge_has(s))
            def _():
                edge_arrival(ph, 1, s).wait_recv()
                total = own[s, pl.ds(mine(s), half)].astype(F32) + e1[ph, s].astype(F32)
                total = total + e2[ph, s].astype(F32)
                for b in range(half // ROWS):
                    block = mine(s) // ROWS + b
                    scale = jnp.where(ecnt[0, 0, s] > block, 0.25, 0.0)
                    part = total[b * ROWS : (b + 1) * ROWS] * scale
                    rows_ref[pl.ds(b * ROWS, ROWS)] = part.astype(BF16)
                edge_copy(ph, 2, s, rows_ref).start()

    def edge_finish(ph, dst):
        for s in range(4):
            base = 4 * fr + s * er

            @pl.when(edge_has(s))
            def _():
                edge_arrival(ph, 2, s).wait_recv()
                dst[pl.ds(base + half - mine(s), half)] = e3[ph, s]

            @pl.when(jnp.logical_not(edge_has(s)))
            def _():
                dst[pl.ds(base, er)] = jnp.zeros((er, dst.shape[1]), BF16)

    def face_finish(ph, k, own, dst):
        @pl.when(face_has(k))
        def _():
            face_arrival(ph, k).wait_recv()
            for b in range(fr // ROWS):
                scale = jnp.where(fcnt[0, 0, k] > b, 0.5, 0.0)
                at = pl.ds(b * ROWS, ROWS)
                total = own[k, at].astype(F32) + rf[ph, k, at].astype(F32)
                dst[pl.ds(k * fr + b * ROWS, ROWS)] = (total * scale).astype(BF16)

        @pl.when(jnp.logical_not(face_has(k)))
        def _():
            dst[pl.ds(k * fr, fr)] = jnp.zeros((fr, dst.shape[1]), BF16)

    edge_halves_start(0, edges_hbm)
    for k in (0, 3, 1, 2):

        @pl.when(face_has(k))
        def _():
            face_copy(0, k, faces_hbm.at[k]).start()

    for n in range(3):
        locals_[n].wait()
    lift = exact_dot(l1[...], l2[...])
    l1[...] = lift
    mpart[...] = exact_dot_t(lift, exact_dot(cmat[...], lift))
    scatter_start(0, mpart, mslots)
    locals_[3].wait()
    edge_columns(0, edges)
    sum_and_gather(0, mpart, mslots, mfull)
    gather_wait(1, mfull)
    mfull_inv = invert(mfull[...])
    collective_drain(0, mpart, mslots, mfull)
    l2[...] = mfull_inv

    locals_[4].wait()
    for k in (1, 2):
        face_finish(0, k, faces, res)
    edge_totals(0, edges, res)
    for k in (0, 3):
        face_finish(0, k, faces, res)
    edge_finish(0, res)

    locals_[5].wait()
    coarse = lax.dot_general(basis[...], res[...], COLS0, preferred_element_type=F32)
    bpart[...] = exact_dot_t(l1[...], coarse)
    scatter_start(2, bpart, bslots)
    locals_[6].wait()

    def local_solve(base, count):
        at = pl.ds(pl.multiple_of(base, 128), count)
        acc[at] = jnp.dot(schur[at], res[...], preferred_element_type=F32)

    @pl.loop(0, 2)
    def _(t):
        local_solve(t * (3 * fr), fr)

    sum_and_gather(2, bpart, bslots, bfull)

    @pl.loop(0, 3)
    def _(t):
        local_solve(jnp.where(t == 0, 4 * fr, t * fr), fr)

    local_solve(5 * fr, 4 * er - fr)

    gather_wait(3, bfull)
    middle = exact_dot(l2[...], bfull[...])
    node = exact_dot(l1[...], middle).astype(BF16)

    def add_coarse(base, count):
        at = pl.ds(base, count)
        return (acc[at] + jnp.dot(basis[at], node, preferred_element_type=F32)).astype(BF16)

    for s in range(4):
        edges[s] = add_coarse(4 * fr + s * er, er)
    for k in (0, 3, 1, 2):
        corr[k] = add_coarse(k * fr, fr)
        if k == 0:
            for s in range(4):

                @pl.when(edge_has(s))
                def _():
                    edge_copy(0, 0, s, edges_hbm.at[s, pl.ds(half - mine(s), half)]).wait_send()

            edge_halves_start(1, edges)

        @pl.when(face_has(k))
        def _():
            face_copy(1, k, corr.at[k]).start()

    edge_columns(1, edges)

    def put_face(k):
        return pltpu.make_async_copy(out.at[pl.ds(k * fr, fr)], outf_hbm.at[k], osem.at[k])

    def put_edge(s):
        return pltpu.make_async_copy(
            out.at[pl.ds(4 * fr + s * er, er)], oute_hbm.at[s], osem.at[4 + s]
        )

    for k in (1, 2):
        face_finish(1, k, corr, out)
        put_face(k).start()
    edge_totals(1, edges, out)
    for k in (0, 3):
        face_finish(1, k, corr, out)
        put_face(k).start()
    edge_finish(1, out)
    for s in range(4):
        put_edge(s).start()

    collective_drain(2, bpart, bslots, bfull)
    for ph in range(2):
        for k in range(4):

            @pl.when(face_has(k))
            def _():
                face_copy(ph, k, faces_hbm.at[k] if ph == 0 else corr.at[k]).wait_send()

        for s in range(4):

            @pl.when(edge_has(s))
            def _():
                if ph:
                    edge_copy(1, 0, s, edges.at[s, pl.ds(half - mine(s), half)]).wait_send()
                edge_copy(ph, 1, s, cs.at[ph, s]).wait_send()
                edge_copy(
                    ph, 2, s, (out if ph else res).at[pl.ds(4 * fr + s * er + mine(s), half)]
                ).wait_send()

    for k in range(4):
        put_face(k).wait()
        put_edge(k).wait()


def body(
    face_pieces,
    edge_pieces,
    face_counts,
    edge_counts,
    schur_inv,
    coarse_basis,
    coarse_mat,
    lift_one,
    lift_two,
):
    gx, gy = lax.axis_size("gx"), lax.axis_size("gy")
    faces, edges = face_pieces[0, 0], edge_pieces[0, 0]
    fr, vec = faces.shape[1:]
    er = edges.shape[1]
    ni, nc = coarse_basis.shape[2:]
    rows = max(16, nc // gy)
    half = er // 2
    anywhere = pl.BlockSpec(memory_space=pl.ANY)
    smem = pl.BlockSpec(memory_space=pltpu.SMEM)
    dma = pltpu.SemaphoreType.DMA
    out_faces, out_edges = pl.pallas_call(
        functools.partial(kernel, gx, gy, rows),
        out_shape=(
            jax.ShapeDtypeStruct(faces.shape, BF16),
            jax.ShapeDtypeStruct(edges.shape, BF16),
        ),
        in_specs=[anywhere, anywhere, smem, smem] + [anywhere] * 5,
        out_specs=(anywhere, anywhere),
        scratch_shapes=[
            pltpu.VMEM(faces.shape, BF16),
            pltpu.VMEM(edges.shape, BF16),
            pltpu.VMEM((ni, ni), BF16),
            pltpu.VMEM((ni, nc), BF16),
            pltpu.VMEM((nc, nc), F32),
            pltpu.VMEM((nc, nc), F32),
            pltpu.VMEM((nc, nc), F32),
            pltpu.VMEM((2, 4, fr, vec), BF16),
            pltpu.VMEM((2, 4, half, vec), BF16),
            pltpu.VMEM((2, 4, half, vec), BF16),
            pltpu.VMEM((2, 4, half, vec), BF16),
            pltpu.VMEM((2, 4, half, vec), BF16),
            pltpu.VMEM((ni, vec), BF16),
            pltpu.VMEM((ni, vec), F32),
            pltpu.VMEM(faces.shape, BF16),
            pltpu.VMEM((ni, vec), BF16),
            pltpu.VMEM((nc, nc), F32),
            pltpu.VMEM((gy, rows, nc), F32),
            pltpu.VMEM((nc, nc), F32),
            pltpu.VMEM((nc, vec), F32),
            pltpu.VMEM((gy, rows, vec), F32),
            pltpu.VMEM((nc, vec), F32),
            dma((7,)),
            dma((2, 4)),
            dma((2, 4)),
            dma((2, 3, 4)),
            dma((2, 3, 4)),
            dma((4, gy)),
            dma((4, gy)),
            dma((8,)),
        ],
        compiler_params=pltpu.CompilerParams(
            collective_id=0, has_side_effects=True, vmem_limit_bytes=62 * 2**20
        ),
        cost_estimate=pl.CostEstimate(
            flops=2 * ni * vec * (ni + 2 * nc), bytes_accessed=2 * ni * (ni + 3 * vec), transcendentals=0
        ),
    )(
        faces,
        edges,
        face_counts,
        edge_counts,
        schur_inv[0, 0],
        coarse_basis[0, 0],
        coarse_mat[0, 0],
        lift_one[0, 0],
        lift_two[0, 0],
    )
    return out_faces[None, None], out_edges[None, None]


def solution(mesh):
    return jax.shard_map(
        body,
        mesh=mesh,
        in_specs=(
            P("gx", "gy", None, None, None),
            P("gx", "gy", None, None, None),
            P("gx", "gy", None),
            P("gx", "gy", None),
            P("gx", "gy", None, None),
            P("gx", "gy", None, None),
            P("gx", "gy", None, None),
            P("gx", "gy", None, None),
            P("gx", "gy", None, None),
        ),
        out_specs=(P("gx", "gy", None, None, None), P("gx", "gy", None, None, None)),
        check_vma=False,
    )
```

```python
import functools

import jax
import jax.numpy as jnp
from jax import lax
from jax.experimental import pallas as pl
from jax.experimental.pallas import tpu as pltpu
from jax.sharding import PartitionSpec as P

ROWS = 64
F32 = jnp.float32
BF16 = jnp.bfloat16
MESH = pl.DeviceIdType.MESH
HIGHEST = lax.Precision.HIGHEST
FACE_STEP = ((-1, 0), (0, -1), (0, 1), (1, 0))
EDGE_STEP = ((-1, -1), (-1, 1), (1, -1), (1, 1))
COLS0 = (((0,), (0,)), ((), ()))


def exact_dot(a, b):
    return jnp.dot(a, b, precision=HIGHEST, preferred_element_type=F32)


def exact_dot_t(a, b):
    return lax.dot_general(a, b, COLS0, precision=HIGHEST, preferred_element_type=F32)


def invert(matrix):
    size = matrix.shape[0]
    block = 8
    lane = lax.broadcasted_iota(jnp.int32, (1, size), 1)

    def step(_, a):
        cols = [jnp.broadcast_to(a[:, t : t + 1], (size, size)) for t in range(block)]
        d = [[cols[t][s : s + 1] for t in range(block)] for s in range(block)]
        w = [
            jnp.where(lane < block, jnp.where(lane == s, 1.0, 0.0), a[s : s + 1])
            for s in range(block)
        ]
        for p in range(0, block, 2):
            q = p + 1
            inv = 1.0 / (d[p][p] * d[q][q] - d[p][q] * d[q][p])
            i00, i01 = d[q][q] * inv, d[p][q] * inv
            i10, i11 = d[q][p] * inv, d[p][p] * inv
            w[p], w[q] = i00 * w[p] - i01 * w[q], i11 * w[q] - i10 * w[p]
            for t in range(q + 1, block):
                d[p][t], d[q][t] = i00 * d[p][t] - i01 * d[q][t], i11 * d[q][t] - i10 * d[p][t]
            for s in range(block):
                if s not in (p, q):
                    f, g = d[s][p], d[s][q]
                    w[s] = w[s] - f * w[p] - g * w[q]
                    for t in range(q + 1, block):
                        d[s][t] = d[s][t] - f * d[p][t] - g * d[q][t]
        rest = jnp.where(lane < block, 0.0, a[block:])
        for t in range(block):
            rest = rest - cols[t][block:] * w[t]
        return pltpu.roll(jnp.concatenate([rest] + w, axis=0), size - block, 1)

    return lax.fori_loop(0, size // block, step, matrix)


def kernel(
    gx,
    gy,
    rows,
    faces_hbm,
    edges_hbm,
    fcnt,
    ecnt,
    schur_hbm,
    basis_hbm,
    cmat_hbm,
    l1_hbm,
    l2_hbm,
    outf_hbm,
    oute_hbm,
    faces,
    edges,
    schur,
    basis,
    cmat,
    l1,
    l2,
    rf,
    e1,
    e2,
    e3,
    cs,
    res,
    acc,
    corr,
    out,
    mpart,
    mslots,
    mfull,
    bpart,
    bslots,
    bfull,
    local_sem,
    fsend,
    frecv,
    esend,
    erecv,
    csend,
    crecv,
    osem,
):
    i = lax.axis_index("gx")
    j = lax.axis_index("gy")
    fr = faces.shape[1]
    er = edges.shape[1]
    half = er // 2
    nc = mpart.shape[0]
    owners = nc // rows

    locals_ = [
        pltpu.make_async_copy(src, dst, local_sem.at[n])
        for n, (src, dst) in enumerate(
            (
                (l1_hbm, l1),
                (l2_hbm, l2),
                (cmat_hbm, cmat),
                (edges_hbm, edges),
                (faces_hbm, faces),
                (basis_hbm, basis),
                (schur_hbm, schur),
            )
        )
    ]
    for copy in locals_:
        copy.start()

    has = {-1: i > 0, 1: i < gx - 1}
    hasy = {-1: j > 0, 1: j < gy - 1}

    def peer(d):
        return lax.rem(j + d, gy)

    barrier = pltpu.get_barrier_semaphore()
    for d in range(1, gy):
        pl.semaphore_signal(barrier, inc=1, device_id=(i, peer(d)), device_id_type=MESH)
    for a in (-1, 1):

        @pl.when(has[a])
        def _():
            pl.semaphore_signal(barrier, inc=1, device_id=(i + a, j), device_id_type=MESH)

    pl.semaphore_wait(barrier, gy - 1 + has[-1].astype(jnp.int32) + has[1].astype(jnp.int32))

    def remote(src, dst, ssem, rsem, target):
        return pltpu.make_async_remote_copy(
            src_ref=src,
            dst_ref=dst,
            send_sem=ssem,
            recv_sem=rsem,
            device_id=target,
            device_id_type=MESH,
        )

    def face_has(k):
        a, b = FACE_STEP[k]
        return has[a] if a else hasy[b]

    def face_copy(ph, k, src):
        a, b = FACE_STEP[k]
        return remote(src, rf.at[ph, 3 - k], fsend.at[ph, k], frecv.at[ph, 3 - k], (i + a, j + b))

    def face_arrival(ph, k):
        a, b = FACE_STEP[k]
        return remote(rf.at[ph, k], rf.at[ph, k], fsend.at[ph, k], frecv.at[ph, k], (i + a, j + b))

    def edge_has(s):
        a, b = EDGE_STEP[s]
        return has[a] & hasy[b]

    def mine(s):
        return 0 if s % 2 else half

    def edge_copy(ph, stage, s, src):
        a, b = EDGE_STEP[s]
        land, flip, target = (
            (e1, s ^ 1, (i, j + b)),
            (e2, s ^ 2, (i + a, j)),
            (e3, s ^ 1, (i, j + b)),
        )[stage]
        return remote(
            src, land.at[ph, flip], esend.at[ph, stage, s], erecv.at[ph, stage, flip], target
        )

    def edge_arrival(ph, stage, s):
        a, b = EDGE_STEP[s]
        land = (e1, e2, e3)[stage]
        target = (i + a, j) if stage == 1 else (i, j + b)
        ref = land.at[ph, s]
        return remote(ref, ref, esend.at[ph, stage, s], erecv.at[ph, stage, s], target)

    def owned_by(index):
        return True if owners >= gy else index < owners

    def guarded(cond, fn):
        if cond is True:
            fn()
        else:
            pl.when(cond)(fn)

    def part_rows(ref, index):
        return ref.at[pl.ds(pl.multiple_of(index * rows, rows), rows)]

    def scatter_copy(which, src, slots, d):
        p = peer(d)
        return remote(
            part_rows(src, jnp.minimum(p, owners - 1)), slots.at[d], csend.at[which, d], crecv.at[which, d], (i, p)
        )

    def scatter_start(which, src, slots):
        for d in range(1, gy):
            guarded(owned_by(peer(d)), lambda: scatter_copy(which, src, slots, d).start())

    def gather_copy(which, full, d):
        ref = part_rows(full, jnp.minimum(j, owners - 1))
        return remote(ref, ref, csend.at[which, d], crecv.at[which, d], (i, peer(d)))

    def sum_and_gather(which, src, slots, full):
        def go():
            total = part_rows(src, jnp.minimum(j, owners - 1))[...]
            for d in range(1, gy):
                scatter_copy(which, src, slots, d).wait_recv()
                total = total + slots[d]
            part_rows(full, jnp.minimum(j, owners - 1))[...] = total
            for d in range(1, gy):
                gather_copy(which + 1, full, d).start()

        guarded(owned_by(j), go)

    def gather_wait(which, full):
        for d in range(1, gy):
            q = lax.rem(j - d + gy, gy)

            def wait():
                ref = part_rows(full, jnp.minimum(q, owners - 1))
                remote(ref, ref, csend.at[which, d], crecv.at[which, d], (i, q)).wait_recv()

            guarded(owned_by(q), wait)

    def collective_drain(which, src, slots, full):
        for d in range(1, gy):
            guarded(owned_by(peer(d)), lambda: scatter_copy(which, src, slots, d).wait_send())
            guarded(owned_by(j), lambda: gather_copy(which + 1, full, d).wait_send())

    def edge_halves_start(ph, src):
        for s in range(4):

            @pl.when(edge_has(s))
            def _():
                edge_copy(ph, 0, s, src.at[s, pl.ds(half - mine(s), half)]).start()

    def edge_columns(ph, own):
        for s in range(4):

            @pl.when(edge_has(s))
            def _():
                edge_arrival(ph, 0, s).wait_recv()
                total = own[s, pl.ds(mine(s), half)].astype(F32) + e1[ph, s].astype(F32)
                cs[ph, s] = total.astype(BF16)
                edge_copy(ph, 1, s, cs.at[ph, s]).start()

    def edge_totals(ph, own, dst):
        for s in range(4):
            rows_ref = dst.at[pl.ds(4 * fr + s * er + mine(s), half)]

            @pl.when(edge_has(s))
            def _():
                edge_arrival(ph, 1, s).wait_recv()
                total = own[s, pl.ds(mine(s), half)].astype(F32) + e1[ph, s].astype(F32)
                total = total + e2[ph, s].astype(F32)
                for b in range(half // ROWS):
                    block = mine(s) // ROWS + b
                    scale = jnp.where(ecnt[0, 0, s] > block, 0.25, 0.0)
                    part = total[b * ROWS : (b + 1) * ROWS] * scale
                    rows_ref[pl.ds(b * ROWS, ROWS)] = part.astype(BF16)
                edge_copy(ph, 2, s, rows_ref).start()

    def edge_finish(ph, dst):
        for s in range(4):
            base = 4 * fr + s * er

            @pl.when(edge_has(s))
            def _():
                edge_arrival(ph, 2, s).wait_recv()
                dst[pl.ds(base + half - mine(s), half)] = e3[ph, s]

            @pl.when(jnp.logical_not(edge_has(s)))
            def _():
                dst[pl.ds(base, er)] = jnp.zeros((er, dst.shape[1]), BF16)

    def face_finish(ph, k, own, dst):
        @pl.when(face_has(k))
        def _():
            face_arrival(ph, k).wait_recv()
            for b in range(fr // ROWS):
                scale = jnp.where(fcnt[0, 0, k] > b, 0.5, 0.0)
                at = pl.ds(b * ROWS, ROWS)
                total = own[k, at].astype(F32) + rf[ph, k, at].astype(F32)
                dst[pl.ds(k * fr + b * ROWS, ROWS)] = (total * scale).astype(BF16)

        @pl.when(jnp.logical_not(face_has(k)))
        def _():
            dst[pl.ds(k * fr, fr)] = jnp.zeros((fr, dst.shape[1]), BF16)

    edge_halves_start(0, edges_hbm)
    def pieces_start(ks):
        for k in ks:

            @pl.when(face_has(k))
            def _():
                face_copy(0, k, faces_hbm.at[k]).start()

    pieces_start((0, 3))

    for n in range(3):
        locals_[n].wait()
    lift = exact_dot(l1[...], l2[...])
    l1[...] = lift
    mpart[...] = exact_dot_t(lift, exact_dot(cmat[...], lift))
    scatter_start(0, mpart, mslots)
    locals_[3].wait()
    edge_columns(0, edges)
    sum_and_gather(0, mpart, mslots, mfull)
    pieces_start((1, 2))
    gather_wait(1, mfull)
    mfull_inv = invert(mfull[...])
    collective_drain(0, mpart, mslots, mfull)
    l2[...] = mfull_inv

    locals_[4].wait()
    edge_totals(0, edges, res)
    for k in (0, 3, 1, 2):
        face_finish(0, k, faces, res)
    edge_finish(0, res)

    locals_[5].wait()
    coarse = lax.dot_general(basis[...], res[...], COLS0, preferred_element_type=F32)
    bpart[...] = exact_dot_t(l1[...], coarse)
    scatter_start(2, bpart, bslots)
    locals_[6].wait()

    def local_solve(base, count):
        at = pl.ds(pl.multiple_of(base, 128), count)
        acc[at] = jnp.dot(schur[at], res[...], preferred_element_type=F32)

    @pl.loop(0, 2)
    def _(t):
        local_solve(t * (3 * fr), fr)

    sum_and_gather(2, bpart, bslots, bfull)

    @pl.loop(0, 3)
    def _(t):
        local_solve(jnp.where(t == 0, 4 * fr, t * fr), fr)

    local_solve(5 * fr, 4 * er - fr)

    gather_wait(3, bfull)
    middle = exact_dot(l2[...], bfull[...])
    node = exact_dot(l1[...], middle).astype(BF16)

    def add_coarse(base, count):
        at = pl.ds(base, count)
        return (acc[at] + jnp.dot(basis[at], node, preferred_element_type=F32)).astype(BF16)

    for s in range(4):
        edges[s] = add_coarse(4 * fr + s * er, er)
    for k in (0, 3, 1, 2):
        corr[k] = add_coarse(k * fr, fr)
        if k == 0:
            for s in range(4):

                @pl.when(edge_has(s))
                def _():
                    edge_copy(0, 0, s, edges_hbm.at[s, pl.ds(half - mine(s), half)]).wait_send()

            edge_halves_start(1, edges)

        @pl.when(face_has(k))
        def _():
            face_copy(1, k, corr.at[k]).start()

    edge_columns(1, edges)

    def put_face(k):
        return pltpu.make_async_copy(out.at[pl.ds(k * fr, fr)], outf_hbm.at[k], osem.at[k])

    def put_edge(s):
        return pltpu.make_async_copy(
            out.at[pl.ds(4 * fr + s * er, er)], oute_hbm.at[s], osem.at[4 + s]
        )

    for k in (1, 2):
        face_finish(1, k, corr, out)
        put_face(k).start()
    edge_totals(1, edges, out)
    for k in (0, 3):
        face_finish(1, k, corr, out)
        put_face(k).start()
    edge_finish(1, out)
    for s in range(4):
        put_edge(s).start()

    collective_drain(2, bpart, bslots, bfull)
    for ph in range(2):
        for k in range(4):

            @pl.when(face_has(k))
            def _():
                face_copy(ph, k, faces_hbm.at[k] if ph == 0 else corr.at[k]).wait_send()

        for s in range(4):

            @pl.when(edge_has(s))
            def _():
                if ph:
                    edge_copy(1, 0, s, edges.at[s, pl.ds(half - mine(s), half)]).wait_send()
                edge_copy(ph, 1, s, cs.at[ph, s]).wait_send()
                edge_copy(
                    ph, 2, s, (out if ph else res).at[pl.ds(4 * fr + s * er + mine(s), half)]
                ).wait_send()

    for k in range(4):
        put_face(k).wait()
        put_edge(k).wait()


def body(
    face_pieces,
    edge_pieces,
    face_counts,
    edge_counts,
    schur_inv,
    coarse_basis,
    coarse_mat,
    lift_one,
    lift_two,
):
    gx, gy = lax.axis_size("gx"), lax.axis_size("gy")
    faces, edges = face_pieces[0, 0], edge_pieces[0, 0]
    fr, vec = faces.shape[1:]
    er = edges.shape[1]
    ni, nc = coarse_basis.shape[2:]
    rows = max(16, nc // gy)
    half = er // 2
    anywhere = pl.BlockSpec(memory_space=pl.ANY)
    smem = pl.BlockSpec(memory_space=pltpu.SMEM)
    dma = pltpu.SemaphoreType.DMA
    out_faces, out_edges = pl.pallas_call(
        functools.partial(kernel, gx, gy, rows),
        out_shape=(
            jax.ShapeDtypeStruct(faces.shape, BF16),
            jax.ShapeDtypeStruct(edges.shape, BF16),
        ),
        in_specs=[anywhere, anywhere, smem, smem] + [anywhere] * 5,
        out_specs=(anywhere, anywhere),
        scratch_shapes=[
            pltpu.VMEM(faces.shape, BF16),
            pltpu.VMEM(edges.shape, BF16),
            pltpu.VMEM((ni, ni), BF16),
            pltpu.VMEM((ni, nc), BF16),
            pltpu.VMEM((nc, nc), F32),
            pltpu.VMEM((nc, nc), F32),
            pltpu.VMEM((nc, nc), F32),
            pltpu.VMEM((2, 4, fr, vec), BF16),
            pltpu.VMEM((2, 4, half, vec), BF16),
            pltpu.VMEM((2, 4, half, vec), BF16),
            pltpu.VMEM((2, 4, half, vec), BF16),
            pltpu.VMEM((2, 4, half, vec), BF16),
            pltpu.VMEM((ni, vec), BF16),
            pltpu.VMEM((ni, vec), F32),
            pltpu.VMEM(faces.shape, BF16),
            pltpu.VMEM((ni, vec), BF16),
            pltpu.VMEM((nc, nc), F32),
            pltpu.VMEM((gy, rows, nc), F32),
            pltpu.VMEM((nc, nc), F32),
            pltpu.VMEM((nc, vec), F32),
            pltpu.VMEM((gy, rows, vec), F32),
            pltpu.VMEM((nc, vec), F32),
            dma((7,)),
            dma((2, 4)),
            dma((2, 4)),
            dma((2, 3, 4)),
            dma((2, 3, 4)),
            dma((4, gy)),
            dma((4, gy)),
            dma((8,)),
        ],
        compiler_params=pltpu.CompilerParams(
            collective_id=0, has_side_effects=True, vmem_limit_bytes=62 * 2**20
        ),
        cost_estimate=pl.CostEstimate(
            flops=2 * ni * vec * (ni + 2 * nc), bytes_accessed=2 * ni * (ni + 3 * vec), transcendentals=0
        ),
    )(
        faces,
        edges,
        face_counts,
        edge_counts,
        schur_inv[0, 0],
        coarse_basis[0, 0],
        coarse_mat[0, 0],
        lift_one[0, 0],
        lift_two[0, 0],
    )
    return out_faces[None, None], out_edges[None, None]


def solution(mesh):
    return jax.shard_map(
        body,
        mesh=mesh,
        in_specs=(
            P("gx", "gy", None, None, None),
            P("gx", "gy", None, None, None),
            P("gx", "gy", None),
            P("gx", "gy", None),
            P("gx", "gy", None, None),
            P("gx", "gy", None, None),
            P("gx", "gy", None, None),
            P("gx", "gy", None, None),
            P("gx", "gy", None, None),
        ),
        out_specs=(P("gx", "gy", None, None, None), P("gx", "gy", None, None, None)),
        check_vma=False,
    )
```

```python
import functools

import jax
import jax.numpy as jnp
from jax import lax
from jax.experimental import pallas as pl
from jax.experimental.pallas import tpu as pltpu
from jax.sharding import PartitionSpec as P

ROWS = 64
F32 = jnp.float32
BF16 = jnp.bfloat16
MESH = pl.DeviceIdType.MESH
HIGHEST = lax.Precision.HIGHEST
FACE_STEP = ((-1, 0), (0, -1), (0, 1), (1, 0))
EDGE_STEP = ((-1, -1), (-1, 1), (1, -1), (1, 1))
COLS0 = (((0,), (0,)), ((), ()))


def exact_dot(a, b):
    return jnp.dot(a, b, precision=HIGHEST, preferred_element_type=F32)


def exact_dot_t(a, b):
    return lax.dot_general(a, b, COLS0, precision=HIGHEST, preferred_element_type=F32)


def invert(matrix):
    size = matrix.shape[0]
    block = 8
    lane = lax.broadcasted_iota(jnp.int32, (1, size), 1)

    def step(_, a):
        cols = [jnp.broadcast_to(a[:, t : t + 1], (size, size)) for t in range(block)]
        d = [[cols[t][s : s + 1] for t in range(block)] for s in range(block)]
        w = [
            jnp.where(lane < block, jnp.where(lane == s, 1.0, 0.0), a[s : s + 1])
            for s in range(block)
        ]
        for p in range(0, block, 2):
            q = p + 1
            inv = 1.0 / (d[p][p] * d[q][q] - d[p][q] * d[q][p])
            i00, i01 = d[q][q] * inv, d[p][q] * inv
            i10, i11 = d[q][p] * inv, d[p][p] * inv
            w[p], w[q] = i00 * w[p] - i01 * w[q], i11 * w[q] - i10 * w[p]
            for t in range(q + 1, block):
                d[p][t], d[q][t] = i00 * d[p][t] - i01 * d[q][t], i11 * d[q][t] - i10 * d[p][t]
            for s in range(block):
                if s not in (p, q):
                    f, g = d[s][p], d[s][q]
                    w[s] = w[s] - f * w[p] - g * w[q]
                    for t in range(q + 1, block):
                        d[s][t] = d[s][t] - f * d[p][t] - g * d[q][t]
        rest = jnp.where(lane < block, 0.0, a[block:])
        for t in range(block):
            rest = rest - cols[t][block:] * w[t]
        return pltpu.roll(jnp.concatenate([rest] + w, axis=0), size - block, 1)

    return lax.fori_loop(0, size // block, step, matrix)


def kernel(
    gx,
    gy,
    rows,
    faces_hbm,
    edges_hbm,
    fcnt,
    ecnt,
    schur_hbm,
    basis_hbm,
    cmat_hbm,
    l1_hbm,
    l2_hbm,
    outf_hbm,
    oute_hbm,
    faces,
    edges,
    schur,
    basis,
    cmat,
    l1,
    l2,
    rf,
    e1,
    e2,
    e3,
    cs,
    res,
    acc,
    corr,
    out,
    mpart,
    mslots,
    mfull,
    bpart,
    bslots,
    bfull,
    local_sem,
    fsend,
    frecv,
    esend,
    erecv,
    csend,
    crecv,
    osem,
):
    i = lax.axis_index("gx")
    j = lax.axis_index("gy")
    fr = faces.shape[1]
    er = edges.shape[1]
    half = er // 2
    nc = mpart.shape[0]
    owners = nc // rows

    locals_ = [
        pltpu.make_async_copy(src, dst, local_sem.at[n])
        for n, (src, dst) in enumerate(
            (
                (l1_hbm, l1),
                (l2_hbm, l2),
                (cmat_hbm, cmat),
                (edges_hbm, edges),
                (faces_hbm, faces),
                (basis_hbm, basis),
                (schur_hbm, schur),
            )
        )
    ]
    for copy in locals_:
        copy.start()

    has = {-1: i > 0, 1: i < gx - 1}
    hasy = {-1: j > 0, 1: j < gy - 1}

    def peer(d):
        return lax.rem(j + d, gy)

    barrier = pltpu.get_barrier_semaphore()
    for d in range(1, gy):
        pl.semaphore_signal(barrier, inc=1, device_id=(i, peer(d)), device_id_type=MESH)
    for a in (-1, 1):

        @pl.when(has[a])
        def _():
            pl.semaphore_signal(barrier, inc=1, device_id=(i + a, j), device_id_type=MESH)

    pl.semaphore_wait(barrier, gy - 1 + has[-1].astype(jnp.int32) + has[1].astype(jnp.int32))

    def remote(src, dst, ssem, rsem, target):
        return pltpu.make_async_remote_copy(
            src_ref=src,
            dst_ref=dst,
            send_sem=ssem,
            recv_sem=rsem,
            device_id=target,
            device_id_type=MESH,
        )

    def face_has(k):
        a, b = FACE_STEP[k]
        return has[a] if a else hasy[b]

    def face_copy(ph, k, src):
        a, b = FACE_STEP[k]
        return remote(src, rf.at[ph, 3 - k], fsend.at[ph, k], frecv.at[ph, 3 - k], (i + a, j + b))

    def face_arrival(ph, k):
        a, b = FACE_STEP[k]
        return remote(rf.at[ph, k], rf.at[ph, k], fsend.at[ph, k], frecv.at[ph, k], (i + a, j + b))

    def edge_has(s):
        a, b = EDGE_STEP[s]
        return has[a] & hasy[b]

    def mine(s):
        return 0 if s % 2 else half

    def edge_copy(ph, stage, s, src):
        a, b = EDGE_STEP[s]
        land, flip, target = (
            (e1, s ^ 1, (i, j + b)),
            (e2, s ^ 2, (i + a, j)),
            (e3, s ^ 1, (i, j + b)),
        )[stage]
        return remote(
            src, land.at[ph, flip], esend.at[ph, stage, s], erecv.at[ph, stage, flip], target
        )

    def edge_arrival(ph, stage, s):
        a, b = EDGE_STEP[s]
        land = (e1, e2, e3)[stage]
        target = (i + a, j) if stage == 1 else (i, j + b)
        ref = land.at[ph, s]
        return remote(ref, ref, esend.at[ph, stage, s], erecv.at[ph, stage, s], target)

    def owned_by(index):
        return True if owners >= gy else index < owners

    def guarded(cond, fn):
        if cond is True:
            fn()
        else:
            pl.when(cond)(fn)

    def part_rows(ref, index):
        return ref.at[pl.ds(pl.multiple_of(index * rows, rows), rows)]

    def scatter_copy(which, src, slots, d):
        p = peer(d)
        return remote(
            part_rows(src, jnp.minimum(p, owners - 1)), slots.at[d], csend.at[which, d], crecv.at[which, d], (i, p)
        )

    def scatter_start(which, src, slots):
        for d in range(1, gy):
            guarded(owned_by(peer(d)), lambda: scatter_copy(which, src, slots, d).start())

    def gather_copy(which, full, d):
        ref = part_rows(full, jnp.minimum(j, owners - 1))
        return remote(ref, ref, csend.at[which, d], crecv.at[which, d], (i, peer(d)))

    def sum_and_gather(which, src, slots, full):
        def go():
            total = part_rows(src, jnp.minimum(j, owners - 1))[...]
            for d in range(1, gy):
                scatter_copy(which, src, slots, d).wait_recv()
                total = total + slots[d]
            part_rows(full, jnp.minimum(j, owners - 1))[...] = total
            for d in range(1, gy):
                gather_copy(which + 1, full, d).start()

        guarded(owned_by(j), go)

    def gather_wait(which, full):
        for d in range(1, gy):
            q = lax.rem(j - d + gy, gy)

            def wait():
                ref = part_rows(full, jnp.minimum(q, owners - 1))
                remote(ref, ref, csend.at[which, d], crecv.at[which, d], (i, q)).wait_recv()

            guarded(owned_by(q), wait)

    def collective_drain(which, src, slots, full):
        for d in range(1, gy):
            guarded(owned_by(peer(d)), lambda: scatter_copy(which, src, slots, d).wait_send())
            guarded(owned_by(j), lambda: gather_copy(which + 1, full, d).wait_send())

    def edge_halves_start(ph, src):
        for s in range(4):

            @pl.when(edge_has(s))
            def _():
                edge_copy(ph, 0, s, src.at[s, pl.ds(half - mine(s), half)]).start()

    def edge_columns(ph, own):
        for s in range(4):

            @pl.when(edge_has(s))
            def _():
                edge_arrival(ph, 0, s).wait_recv()
                total = own[s, pl.ds(mine(s), half)].astype(F32) + e1[ph, s].astype(F32)
                cs[ph, s] = total.astype(BF16)
                edge_copy(ph, 1, s, cs.at[ph, s]).start()

    def edge_totals(ph, own, dst):
        for s in range(4):
            rows_ref = dst.at[pl.ds(4 * fr + s * er + mine(s), half)]

            @pl.when(edge_has(s))
            def _():
                edge_arrival(ph, 1, s).wait_recv()
                total = own[s, pl.ds(mine(s), half)].astype(F32) + e1[ph, s].astype(F32)
                total = total + e2[ph, s].astype(F32)
                for b in range(half // ROWS):
                    block = mine(s) // ROWS + b
                    scale = jnp.where(ecnt[0, 0, s] > block, 0.25, 0.0)
                    part = total[b * ROWS : (b + 1) * ROWS] * scale
                    rows_ref[pl.ds(b * ROWS, ROWS)] = part.astype(BF16)
                edge_copy(ph, 2, s, rows_ref).start()

    def edge_finish(ph, dst):
        for s in range(4):
            base = 4 * fr + s * er

            @pl.when(edge_has(s))
            def _():
                edge_arrival(ph, 2, s).wait_recv()
                dst[pl.ds(base + half - mine(s), half)] = e3[ph, s]

            @pl.when(jnp.logical_not(edge_has(s)))
            def _():
                dst[pl.ds(base, er)] = jnp.zeros((er, dst.shape[1]), BF16)

    def face_finish(ph, k, own, dst):
        @pl.when(face_has(k))
        def _():
            face_arrival(ph, k).wait_recv()
            for b in range(fr // ROWS):
                scale = jnp.where(fcnt[0, 0, k] > b, 0.5, 0.0)
                at = pl.ds(b * ROWS, ROWS)
                total = own[k, at].astype(F32) + rf[ph, k, at].astype(F32)
                dst[pl.ds(k * fr + b * ROWS, ROWS)] = (total * scale).astype(BF16)

        @pl.when(jnp.logical_not(face_has(k)))
        def _():
            dst[pl.ds(k * fr, fr)] = jnp.zeros((fr, dst.shape[1]), BF16)

    edge_halves_start(0, edges_hbm)
    def pieces_start(ks):
        for k in ks:

            @pl.when(face_has(k))
            def _():
                face_copy(0, k, faces_hbm.at[k]).start()

    pieces_start((0, 3))

    for n in range(3):
        locals_[n].wait()
    lift = exact_dot(l1[...], l2[...])
    l1[...] = lift
    mpart[...] = exact_dot_t(lift, exact_dot(cmat[...], lift))
    scatter_start(0, mpart, mslots)
    locals_[3].wait()
    edge_columns(0, edges)
    sum_and_gather(0, mpart, mslots, mfull)
    pieces_start((1, 2))
    gather_wait(1, mfull)
    mfull_inv = invert(mfull[...])
    collective_drain(0, mpart, mslots, mfull)
    l2[...] = exact_dot(l1[...], mfull_inv)

    locals_[4].wait()
    edge_totals(0, edges, res)
    for k in (0, 3, 1, 2):
        face_finish(0, k, faces, res)
    edge_finish(0, res)

    locals_[5].wait()
    coarse = lax.dot_general(basis[...], res[...], COLS0, preferred_element_type=F32)
    bpart[...] = exact_dot_t(l1[...], coarse)
    scatter_start(2, bpart, bslots)
    locals_[6].wait()

    def local_solve(base, count):
        at = pl.ds(pl.multiple_of(base, 128), count)
        acc[at] = jnp.dot(schur[at], res[...], preferred_element_type=F32)

    @pl.loop(0, 2)
    def _(t):
        local_solve(t * (3 * fr), fr)

    sum_and_gather(2, bpart, bslots, bfull)

    @pl.loop(0, 3)
    def _(t):
        local_solve(jnp.where(t == 0, 4 * fr, t * fr), fr)

    local_solve(5 * fr, 4 * er - fr)

    gather_wait(3, bfull)
    node = exact_dot(l2[...], bfull[...]).astype(BF16)

    def add_coarse(base, count):
        at = pl.ds(base, count)
        return (acc[at] + jnp.dot(basis[at], node, preferred_element_type=F32)).astype(BF16)

    for s in range(4):
        edges[s] = add_coarse(4 * fr + s * er, er)
    for k in (0, 3, 1, 2):
        corr[k] = add_coarse(k * fr, fr)
        if k == 0:
            for s in range(4):

                @pl.when(edge_has(s))
                def _():
                    edge_copy(0, 0, s, edges_hbm.at[s, pl.ds(half - mine(s), half)]).wait_send()

            edge_halves_start(1, edges)

        @pl.when(face_has(k))
        def _():
            face_copy(1, k, corr.at[k]).start()

    edge_columns(1, edges)

    def put_face(k):
        return pltpu.make_async_copy(out.at[pl.ds(k * fr, fr)], outf_hbm.at[k], osem.at[k])

    def put_edge(s):
        return pltpu.make_async_copy(
            out.at[pl.ds(4 * fr + s * er, er)], oute_hbm.at[s], osem.at[4 + s]
        )

    for k in (1, 2):
        face_finish(1, k, corr, out)
        put_face(k).start()
    edge_totals(1, edges, out)
    for k in (0, 3):
        face_finish(1, k, corr, out)
        put_face(k).start()
    edge_finish(1, out)
    for s in range(4):
        put_edge(s).start()

    collective_drain(2, bpart, bslots, bfull)
    for ph in range(2):
        for k in range(4):

            @pl.when(face_has(k))
            def _():
                face_copy(ph, k, faces_hbm.at[k] if ph == 0 else corr.at[k]).wait_send()

        for s in range(4):

            @pl.when(edge_has(s))
            def _():
                if ph:
                    edge_copy(1, 0, s, edges.at[s, pl.ds(half - mine(s), half)]).wait_send()
                edge_copy(ph, 1, s, cs.at[ph, s]).wait_send()
                edge_copy(
                    ph, 2, s, (out if ph else res).at[pl.ds(4 * fr + s * er + mine(s), half)]
                ).wait_send()

    for k in range(4):
        put_face(k).wait()
        put_edge(k).wait()


def body(
    face_pieces,
    edge_pieces,
    face_counts,
    edge_counts,
    schur_inv,
    coarse_basis,
    coarse_mat,
    lift_one,
    lift_two,
):
    gx, gy = lax.axis_size("gx"), lax.axis_size("gy")
    faces, edges = face_pieces[0, 0], edge_pieces[0, 0]
    fr, vec = faces.shape[1:]
    er = edges.shape[1]
    ni, nc = coarse_basis.shape[2:]
    rows = max(16, nc // gy)
    half = er // 2
    anywhere = pl.BlockSpec(memory_space=pl.ANY)
    smem = pl.BlockSpec(memory_space=pltpu.SMEM)
    dma = pltpu.SemaphoreType.DMA
    out_faces, out_edges = pl.pallas_call(
        functools.partial(kernel, gx, gy, rows),
        out_shape=(
            jax.ShapeDtypeStruct(faces.shape, BF16),
            jax.ShapeDtypeStruct(edges.shape, BF16),
        ),
        in_specs=[anywhere, anywhere, smem, smem] + [anywhere] * 5,
        out_specs=(anywhere, anywhere),
        scratch_shapes=[
            pltpu.VMEM(faces.shape, BF16),
            pltpu.VMEM(edges.shape, BF16),
            pltpu.VMEM((ni, ni), BF16),
            pltpu.VMEM((ni, nc), BF16),
            pltpu.VMEM((nc, nc), F32),
            pltpu.VMEM((nc, nc), F32),
            pltpu.VMEM((nc, nc), F32),
            pltpu.VMEM((2, 4, fr, vec), BF16),
            pltpu.VMEM((2, 4, half, vec), BF16),
            pltpu.VMEM((2, 4, half, vec), BF16),
            pltpu.VMEM((2, 4, half, vec), BF16),
            pltpu.VMEM((2, 4, half, vec), BF16),
            pltpu.VMEM((ni, vec), BF16),
            pltpu.VMEM((ni, vec), F32),
            pltpu.VMEM(faces.shape, BF16),
            pltpu.VMEM((ni, vec), BF16),
            pltpu.VMEM((nc, nc), F32),
            pltpu.VMEM((gy, rows, nc), F32),
            pltpu.VMEM((nc, nc), F32),
            pltpu.VMEM((nc, vec), F32),
            pltpu.VMEM((gy, rows, vec), F32),
            pltpu.VMEM((nc, vec), F32),
            dma((7,)),
            dma((2, 4)),
            dma((2, 4)),
            dma((2, 3, 4)),
            dma((2, 3, 4)),
            dma((4, gy)),
            dma((4, gy)),
            dma((8,)),
        ],
        compiler_params=pltpu.CompilerParams(
            collective_id=0, has_side_effects=True, vmem_limit_bytes=62 * 2**20
        ),
        cost_estimate=pl.CostEstimate(
            flops=2 * ni * vec * (ni + 2 * nc), bytes_accessed=2 * ni * (ni + 3 * vec), transcendentals=0
        ),
    )(
        faces,
        edges,
        face_counts,
        edge_counts,
        schur_inv[0, 0],
        coarse_basis[0, 0],
        coarse_mat[0, 0],
        lift_one[0, 0],
        lift_two[0, 0],
    )
    return out_faces[None, None], out_edges[None, None]


def solution(mesh):
    return jax.shard_map(
        body,
        mesh=mesh,
        in_specs=(
            P("gx", "gy", None, None, None),
            P("gx", "gy", None, None, None),
            P("gx", "gy", None),
            P("gx", "gy", None),
            P("gx", "gy", None, None),
            P("gx", "gy", None, None),
            P("gx", "gy", None, None),
            P("gx", "gy", None, None),
            P("gx", "gy", None, None),
        ),
        out_specs=(P("gx", "gy", None, None, None), P("gx", "gy", None, None, None)),
        check_vma=False,
    )
```
